32 devices in a mesh: groups: 2 (over y), row: 4 (over x, core), col: 4 (over z).
Axes of the slice: x: 2, y: 2, z: 4, core: 2. Of those that a mesh axis runs over, the one named last changes fastest.
Arguments:
- basis_values: bfloat16 [4, 4, 2048, 1536], P('row', 'col'), may hold values from -6 to 6
- potential: float32 [4, 4, 2048], P('row', 'col'), may hold values from -0.125 to 0.125
- basis_blocks: int32 [4, 4, 12], P('row', 'col'), may hold values from 0 to 63, as said below
- factor: bfloat16 [16, 4, 128, 1024], P(None, 'row', None, 'col'), may hold values from -0.1875 to 0.1875
Outputs:
- hamiltonian: float32 [32, 4, 16, 4, 128, 128], P('groups', 'row', None, 'col'), parts along dimension 0
- product: float32 [32, 4, 128, 16, 4, 128], P('groups', 'row', None, None, 'col'), parts along dimension 0
The draws below stay inside these ranges and needn't reach their ends.
There are 2 independent parts, one for each index of `groups`. The reference program is written for one: setup_inputs(seed, part) draws one part's arguments, and reference() takes and returns one part's arrays. A program takes and returns all parts, laid end to end along the dimension named above; an argument that names none is the same for every part. Nothing has to cross between parts.
Inputs may be any that keep to these rules, and one draw needn't show every extreme that they name: `basis_blocks`: the 12 blocks of one batch are distinct and lie within 16 consecutive blocks counted cyclically over the 64 blocks of the window; every such range starts at one common offset modulo 16, and every block of the range whose position in it is a multiple of 4 is on the list. Hence at most 16 of a batch's block pairs (I, J) share the same (I mod 4, J mod 4), and some pair of residues has exactly 16.
All inputs are finite; a program needn't handle non-finite values.
Results may differ from the reference program's by a relative error of at most 0.0048.
Values may be sent and summed in bfloat16 or wider, within the bound.
A program may use at most 128 MiB of HBM per device.

```python
import jax
import jax.numpy as jnp
from jax import lax

NB = 8192
BS = 128
WIN = 16
G = 2048
KB = 8
LB = 12
NBLK = 64
L = 1536
GRID_ROWS = 4
GRID_COLS = 4
LOC_ROWS = 16
LOC_COLS = 16
KW = 1024


def draw_basis_blocks(key, part):
    key_window = jax.random.fold_in(key, 11)
    key_offset = jax.random.fold_in(key, 23)
    key_drop = jax.random.fold_in(key, 37)
    window = jax.random.randint(key_window, (GRID_ROWS, GRID_COLS, 1, 1), 0, NBLK // WIN)
    offset = jax.random.randint(key_offset, (), 0, WIN)
    dropped = jax.random.randint(key_drop, (GRID_ROWS, GRID_COLS, WIN // 4, 1), 1, 4)
    second = jnp.where(dropped == 1, 2, 1)
    third = jnp.where(dropped == 3, 2, 3)
    first = jnp.zeros_like(dropped)
    within = jnp.concatenate([first, second, third], axis=3)
    base = 4 * jnp.arange(WIN // 4)[None, None, :, None]
    blocks = (WIN * window + offset + base + within) % NBLK
    return blocks.reshape(GRID_ROWS, GRID_COLS, LB).astype(jnp.int32)


def shard_levels(key, shape, pieces, smallest, high):
    def one(axis_at, parts):
        draws = jax.random.uniform(jax.random.fold_in(jax.random.fold_in(key, 6), axis_at), (parts,), jnp.float32, smallest / len(pieces), high / len(pieces))
        return jnp.repeat(jnp.exp(draws), shape[axis_at] // parts).reshape((-1,) + (1,) * (len(shape) - axis_at - 1))

    loudness = one(*pieces[0])
    for cut in pieces[1:]:
        loudness = loudness * one(*cut)
    return loudness


def noise(own_key, dims, scale, limit, shards=(), dtype=jnp.bfloat16):
    drawn = scale * jax.random.normal(own_key, dims, jnp.float32)
    if shards:
        drawn = drawn * shard_levels(own_key, dims, shards, -0.22, 0.18)
    return jnp.clip(drawn, -limit, limit).astype(dtype)


def setup_inputs(seed: int = 0, part: int = 0) -> dict:
    key_of = jax.random.split(jax.random.key(seed), 5)
    basis_values = noise(key_of[0], (GRID_ROWS, GRID_COLS, G, L), 1.0, 6.0, ((0, 4), (1, 4)))
    potential = noise(key_of[1], (GRID_ROWS, GRID_COLS, G), G ** -0.5, 0.125, ((0, 4), (1, 4)), jnp.float32)
    basis_blocks = draw_basis_blocks(jax.random.fold_in(key_of[4], 71), part)
    factor = noise(key_of[3], (LOC_ROWS, GRID_ROWS, BS, KW), KW ** -0.5, 0.1875, ((1, 4), (3, 4)))
    return {"basis_values": basis_values, "potential": potential, "basis_blocks": basis_blocks, "factor": factor}


def reference(basis_values, potential, basis_blocks, factor):
    device_count = GRID_ROWS * GRID_COLS
    values = basis_values.reshape(device_count, G, LB * BS)
    weights = potential.reshape(device_count, G)
    lists = basis_blocks.reshape(device_count, LB).astype(jnp.int32)

    def integrate(hamil, inputs):
        phi_batch, weight_batch, list_batch = inputs
        weighted = (phi_batch.astype(jnp.float32) * weight_batch[:, None]).astype(jnp.bfloat16)
        partial_sum = lax.dot_general(phi_batch, weighted, (((0,), (0,)), ((), ())), preferred_element_type=jnp.float32).astype(jnp.bfloat16)
        partial_sum = lax.optimization_barrier(partial_sum).astype(jnp.float32)
        blocks = partial_sum.reshape(LB, BS, LB, BS).transpose(0, 2, 1, 3)
        hamil = hamil.at[list_batch[:, None], list_batch[None, :]].add(blocks)
        return hamil, None

    start_matrix = jnp.zeros((NBLK, NBLK, BS, BS), jnp.float32)
    hamil, unused = lax.scan(integrate, start_matrix, (values, weights, lists))
    hamiltonian = hamil.reshape(LOC_ROWS, GRID_ROWS, LOC_COLS, GRID_COLS, BS, BS)
    head_rows = hamil[:KB].transpose(0, 2, 1, 3).reshape(KB * BS, NB).astype(jnp.bfloat16)
    full_factor = factor.reshape(NB, KB * BS)
    product = jnp.dot(full_factor, head_rows, preferred_element_type=jnp.float32)
    product = product.reshape(LOC_ROWS, GRID_ROWS, BS, LOC_COLS, GRID_COLS, BS)
    return (hamiltonian, product)
```

```python
import functools

import jax
import jax.numpy as jnp
from jax import lax
from jax.experimental import pallas as pl
from jax.experimental.pallas import tpu as pltpu
from jax.sharding import PartitionSpec as P

NB = 8192
WIN = 16
VMEM_LIMIT = 48 * 1024 * 1024


def pack_kernel(half, info, phi_ref, weight_ref, *refs):
    col_refs = refs[:half]
    out_ref, weighted_ref = refs[half:]
    step = pl.program_id(0)
    bs = out_ref.shape[-1]

    @pl.when(step == 0)
    def _():
        out_ref[...] = jnp.zeros_like(out_ref)
        for j in range(half):
            keep = info[half + j].astype(jnp.float32)
            scaled = col_refs[j][...].astype(jnp.float32) * (weight_ref[...] * keep)
            weighted_ref[:, j * bs : (j + 1) * bs] = scaled.astype(jnp.bfloat16)

    total = lax.dot_general(
        phi_ref[...],
        weighted_ref[...],
        (((0,), (0,)), ((), ())),
        preferred_element_type=jnp.float32,
    ).astype(jnp.bfloat16)
    per_step = phi_ref.shape[1] // bs
    for a in range(per_step):
        row_slot = info[3 * half + step * per_step + a]
        for j in range(half):
            out_ref[row_slot + info[2 * half + j]] = total[
                a * bs : (a + 1) * bs, j * bs : (j + 1) * bs
            ]


def sum_kernel(head_rows, head_cols, info, recv_ref, acc_ref, narrow_ref, head_ref):
    step = pl.program_id(0)
    slots = recv_ref.shape[1]

    @pl.when(step == 0)
    def _():
        acc_ref[...] = jnp.zeros_like(acc_ref)

    at = pl.ds(info[head_rows + step] * slots, slots)
    acc_ref[at] += recv_ref[0].astype(jnp.float32)

    @pl.when(step == pl.num_programs(0) - 1)
    def _():
        narrow_ref[...] = acc_ref[...].astype(jnp.bfloat16)
        for i in range(head_rows):
            for t in range(head_cols):
                head_ref[i * head_cols + t] = acc_ref[info[i] * head_cols + t].astype(jnp.bfloat16)


def place_kernel(cols, local_rows, info, acc_ref, out_ref):
    step = pl.program_id(0)
    out_ref[...] = jnp.zeros_like(out_ref)
    base = info[step] * cols
    for t in range(cols):
        out_ref[0, info[local_rows + step * cols + t]] = acc_ref[base + t]


def fill_kernel(cols, local_rows, info, other_ref, tile_ref, out_ref, wide_ref, sems):
    count = other_ref.shape[0]
    wide_ref[...] = other_ref[...].astype(jnp.float32)

    def copy(n):
        i, t = n // cols, n % cols
        return pltpu.make_async_copy(
            wide_ref.at[info[i] * cols + t],
            out_ref.at[i, info[local_rows + n]],
            sems.at[n],
        )

    for n in range(count):
        copy(n).start()
    for n in range(count):
        copy(n).wait()


def product_kernel(head_count, row_count, cols, info, factor_ref, head_ref, out_ref, mat_ref):
    bs = head_ref.shape[-1]
    groups = 2
    width = groups * cols * bs

    @pl.when(pl.program_id(0) == 0)
    def _():
        for i in range(head_count):
            first = info[i] != 0
            for g in range(groups):
                for t in range(cols):
                    block = head_ref[g, i % row_count, (i // row_count) * cols + t]
                    at = (g * cols + t) * bs
                    rows = pl.ds(i * bs, bs)
                    none = jnp.zeros_like(block)
                    mat_ref[rows, at : at + bs] = jnp.where(first, block, none)
                    mat_ref[rows, width + at : width + at + bs] = jnp.where(first, none, block)

    parts = factor_ref.shape[0]
    rows = factor_ref.shape[1] * factor_ref.shape[2]
    left = jnp.concatenate(
        [factor_ref[k].reshape(rows, factor_ref.shape[3]) for k in range(parts)], axis=1
    )
    total = jnp.dot(left, mat_ref[...], preferred_element_type=jnp.float32)
    out_ref[...] = jnp.zeros_like(out_ref)
    local_cols = out_ref.shape[0] // rows
    for n in range(2 * groups * cols):
        out_ref[pl.ds(info[head_count + n], rows, stride=local_cols), :] = total[
            :, n * bs : (n + 1) * bs
        ]


def local(basis_values, potential, basis_blocks, factor):
    row_count = lax.axis_size("row")
    col_count = lax.axis_size("col")
    group = lax.axis_index("groups")
    my_row = lax.axis_index("row")
    my_col = lax.axis_index("col")
    device_count = row_count * col_count
    phi = basis_values[0, 0]
    points, length = phi.shape
    block_list = basis_blocks[0, 0]
    list_length = block_list.shape[0]
    bs = factor.shape[2]
    total_blocks = NB // bs
    local_rows = total_blocks // row_count
    local_cols = total_blocks // col_count
    windows = total_blocks // WIN
    win_rows = WIN // row_count
    win_cols = WIN // col_count
    cols = win_cols // 2
    half = WIN // 2
    slots = win_rows * cols
    head_count = factor.shape[3] * col_count // bs
    params = functools.partial(pltpu.CompilerParams, vmem_limit_bytes=VMEM_LIMIT)

    factors = lax.all_gather(factor[:, 0], "col", axis=0)

    ahead = (block_list[None, :] - block_list[:, None]) % total_blocks
    is_first = jnp.all(ahead < WIN, axis=1)
    start = jnp.sum(jnp.where(is_first, block_list, 0))
    offset = start % WIN
    window = start // WIN
    window_of = lax.all_gather(window[None], ("row", "col"), axis=0, tiled=True)

    position = (block_list - start) % total_blocks
    half_positions = group * half + jnp.arange(half)
    match = position[None, :] == half_positions[:, None]
    list_index = jnp.sum(jnp.where(match, jnp.arange(list_length)[None, :], 0), axis=1)
    present = jnp.any(match, axis=1).astype(jnp.int32)
    col_slot = (offset + half_positions) % col_count * slots + half_positions // col_count % cols
    row_slot = (
        (offset + position) % row_count * (col_count * slots) + position // row_count * cols
    )
    info = jnp.concatenate([list_index, present, col_slot, row_slot]).astype(jnp.int32)

    width = 2 * bs
    packed = pl.pallas_call(
        functools.partial(pack_kernel, half),
        out_shape=jax.ShapeDtypeStruct((device_count * slots, bs, bs), jnp.bfloat16),
        grid_spec=pltpu.PrefetchScalarGridSpec(
            num_scalar_prefetch=1,
            grid=(length // width,),
            in_specs=[
                pl.BlockSpec((points, width), lambda i, info: (0, i)),
                pl.BlockSpec((points, 1), lambda i, info: (0, 0)),
            ]
            + [
                pl.BlockSpec((points, bs), lambda i, info, j=j: (0, info[j]))
                for j in range(half)
            ],
            out_specs=pl.BlockSpec((device_count * slots, bs, bs), lambda i, info: (0, 0, 0)),
            scratch_shapes=[pltpu.VMEM((points, half * bs), jnp.bfloat16)],
        ),
        compiler_params=params(),
    )(info, phi, potential[0, 0][:, None], *([phi] * half))
    received = lax.all_to_all(
        packed.reshape(device_count, slots, bs, bs),
        ("row", "col"),
        split_axis=0,
        concat_axis=0,
        tiled=True,
    )

    rows_held = jnp.arange(local_rows) * row_count + my_row
    relative = (rows_held - offset) % total_blocks
    row_base = relative // WIN * win_rows + relative % WIN // row_count

    def held_cols(of_window, first, count):
        at = (first + jnp.arange(count)) * col_count + (my_col - offset) % col_count
        return (offset + WIN * of_window[:, None] + at[None, :]) % total_blocks // col_count

    row_window = relative // WIN
    own_cols = held_cols(row_window, group * cols, cols).reshape(-1)
    other_cols = held_cols(row_window, (1 - group) * cols, cols).reshape(-1)

    head_rows = max(1, head_count // row_count)
    sum_info = jnp.concatenate([row_base[:head_rows], window_of])
    acc, narrow, head = pl.pallas_call(
        functools.partial(sum_kernel, head_rows, cols),
        out_shape=(
            jax.ShapeDtypeStruct((windows * slots, bs, bs), jnp.float32),
            jax.ShapeDtypeStruct((windows * slots, bs, bs), jnp.bfloat16),
            jax.ShapeDtypeStruct((head_rows * cols, bs, bs), jnp.bfloat16),
        ),
        grid_spec=pltpu.PrefetchScalarGridSpec(
            num_scalar_prefetch=1,
            grid=(device_count,),
            in_specs=[pl.BlockSpec((1, slots, bs, bs), lambda i, info: (i, 0, 0, 0))],
            out_specs=(
                pl.BlockSpec((windows * slots, bs, bs), lambda i, info: (0, 0, 0)),
                pl.BlockSpec((windows * slots, bs, bs), lambda i, info: (0, 0, 0)),
                pl.BlockSpec((head_rows * cols, bs, bs), lambda i, info: (0, 0, 0)),
            ),
        ),
        compiler_params=params(),
    )(sum_info, received)
    heads = lax.all_gather(head, ("groups", "row"), axis=0)
    heads = heads.reshape(2, row_count, head_rows * cols, bs, bs)
    other = lax.ppermute(narrow, "groups", [(0, 1), (1, 0)])

    tile = pl.pallas_call(
        functools.partial(place_kernel, cols, local_rows),
        out_shape=jax.ShapeDtypeStruct((local_rows, local_cols, bs, bs), jnp.float32),
        grid_spec=pltpu.PrefetchScalarGridSpec(
            num_scalar_prefetch=1,
            grid=(local_rows,),
            in_specs=[pl.BlockSpec((windows * slots, bs, bs), lambda i, info: (0, 0, 0))],
            out_specs=pl.BlockSpec((1, local_cols, bs, bs), lambda i, info: (i, 0, 0, 0)),
        ),
        compiler_params=params(),
        cost_estimate=pl.CostEstimate(
            flops=0, bytes_accessed=4 * local_rows * local_cols * bs * bs, transcendentals=0
        ),
    )(jnp.concatenate([row_base, own_cols]), acc)
    tile = pl.pallas_call(
        functools.partial(fill_kernel, cols, local_rows),
        out_shape=jax.ShapeDtypeStruct((local_rows, local_cols, bs, bs), jnp.float32),
        grid_spec=pltpu.PrefetchScalarGridSpec(
            num_scalar_prefetch=1,
            grid=(),
            in_specs=[
                pl.BlockSpec(memory_space=pltpu.VMEM),
                pl.BlockSpec(memory_space=pl.ANY),
            ],
            out_specs=pl.BlockSpec(memory_space=pl.ANY),
            scratch_shapes=[
                pltpu.VMEM((windows * slots, bs, bs), jnp.float32),
                pltpu.SemaphoreType.DMA((windows * slots,)),
            ],
        ),
        input_output_aliases={2: 0},
        compiler_params=params(),
    )(jnp.concatenate([row_base, other_cols]), other, tile)

    head_window = (jnp.arange(head_count) - offset) % total_blocks // WIN
    in_first = (head_window == head_window[0]).astype(jnp.int32)
    pair = jnp.stack([head_window[0], (head_window[0] + 1) % windows])
    product_cols = held_cols(pair, 0, win_cols).reshape(-1)
    chunk = 2
    part_width = factor.shape[3]
    product = pl.pallas_call(
        functools.partial(product_kernel, head_count, row_count, cols),
        out_shape=jax.ShapeDtypeStruct((local_rows * bs * local_cols, bs), jnp.float32),
        grid_spec=pltpu.PrefetchScalarGridSpec(
            num_scalar_prefetch=1,
            grid=(local_rows // chunk,),
            in_specs=[
                pl.BlockSpec((col_count, chunk, bs, part_width), lambda i, info: (0, i, 0, 0)),
                pl.BlockSpec(heads.shape, lambda i, info: (0, 0, 0, 0, 0)),
            ],
            out_specs=pl.BlockSpec((chunk * bs * local_cols, bs), lambda i, info: (i, 0)),
            scratch_shapes=[pltpu.VMEM((head_count * bs, 2 * win_cols * bs), jnp.bfloat16)],
        ),
        compiler_params=params(),
    )(jnp.concatenate([in_first, product_cols]), factors, heads)

    hamiltonian = tile.reshape(local_rows, 1, local_cols, 1, bs, bs)
    return hamiltonian, product.reshape(local_rows, 1, bs, local_cols, 1, bs)


def solution(mesh):
    return jax.shard_map(
        local,
        mesh=mesh,
        in_specs=(
            P("row", "col", None, None),
            P("row", "col", None),
            P("row", "col", None),
            P(None, "row", None, "col"),
        ),
        out_specs=(
            P("groups", "row", None, "col", None, None),
            P("groups", "row", None, None, "col", None),
        ),
        check_vma=False,
    )
```

```python
import functools

import jax
import jax.numpy as jnp
from jax import lax
from jax.experimental import pallas as pl
from jax.experimental.pallas import tpu as pltpu
from jax.sharding import PartitionSpec as P

NB = 8192
WIN = 16
VMEM_LIMIT = 48 * 1024 * 1024


def pack_kernel(half, extra, info, phi_ref, weight_ref, *refs):
    col_refs = refs[:half]
    out_ref, weighted_ref = refs[half:]
    step = pl.program_id(0)
    bs = out_ref.shape[-1]

    @pl.when(step == 0)
    def _():
        out_ref[...] = jnp.zeros_like(out_ref)
        if extra:
            tag = info[info.shape[0] - 1].astype(jnp.float32)
            out_ref[:, out_ref.shape[1] - extra :, :] = jnp.full(
                (out_ref.shape[0], extra, bs), tag, jnp.float32
            ).astype(jnp.bfloat16)
        for j in range(half):
            keep = info[half + j].astype(jnp.float32)
            scaled = col_refs[j][...].astype(jnp.float32) * (weight_ref[...] * keep)
            weighted_ref[:, j * bs : (j + 1) * bs] = scaled.astype(jnp.bfloat16)

    total = lax.dot_general(
        phi_ref[...],
        weighted_ref[...],
        (((0,), (0,)), ((), ())),
        preferred_element_type=jnp.float32,
    ).astype(jnp.bfloat16)
    per_step = phi_ref.shape[1] // bs
    length = pl.num_programs(0) * per_step
    for a in range(per_step):
        at = step * per_step + a
        device = info[3 * half + at]
        rows = pl.ds(pl.multiple_of(info[3 * half + length + at] * bs, bs), bs)
        for j in range(half):
            out_ref[device + info[2 * half + j], rows, :] = total[
                a * bs : (a + 1) * bs, j * bs : (j + 1) * bs
            ]


def sum_kernel(head_rows, slots, info, recv_ref, *refs):
    acc_ref, narrow_ref, head_ref = refs[-3:]
    step = pl.program_id(0)
    bs = acc_ref.shape[-1]

    @pl.when(step == 0)
    def _():
        acc_ref[...] = jnp.zeros_like(acc_ref)

    sources = recv_ref.shape[0]
    for k in range(sources):
        first = info[head_rows + step * sources + k] * slots
        for n in range(slots):
            acc_ref[first + n] += recv_ref[k, n * bs : (n + 1) * bs, :].astype(jnp.float32)

    @pl.when(step == pl.num_programs(0) - 1)
    def _():
        narrow_ref[...] = acc_ref[...].astype(jnp.bfloat16)
        for i in range(head_rows):
            head_ref[i] = acc_ref[info[i]].astype(jnp.bfloat16)


def place_kernel(local_rows, info, acc_ref, out_ref):
    step = pl.program_id(0)
    out_ref[...] = jnp.zeros_like(out_ref)
    out_ref[0, info[local_rows + step]] = acc_ref[info[step]]


def fill_kernel(narrow_count, wide_count, info, *refs):
    narrow_refs = refs[:narrow_count]
    own_refs = refs[narrow_count : narrow_count + wide_count]
    out_ref, wide_ref, sems = refs[narrow_count + wide_count + 1 :]
    local_rows = out_ref.shape[0]
    for k in range(narrow_count):
        wide_ref[k] = narrow_refs[k][...].astype(jnp.float32)

    def copy(k, i):
        source = wide_ref.at[k] if k < narrow_count else own_refs[k - narrow_count]
        return pltpu.make_async_copy(
            source.at[info[i]],
            out_ref.at[i, info[local_rows * (k + 1) + i]],
            sems.at[k * local_rows + i],
        )

    for k in range(narrow_count + wide_count):
        for i in range(local_rows):
            copy(k, i).start()
    for k in range(narrow_count + wide_count):
        for i in range(local_rows):
            copy(k, i).wait()


def product_kernel(head_count, row_count, cols, info, factor_ref, *refs):
    head_refs = refs[:cols]
    out_ref, mat_ref = refs[cols:]
    bs = out_ref.shape[-1]
    groups = 2
    width = groups * cols * bs

    @pl.when(pl.program_id(0) == 0)
    def _():
        for i in range(head_count):
            first = info[i] != 0
            for g in range(groups):
                for t in range(cols):
                    block = head_refs[t][g, i % row_count, i // row_count]
                    at = (g * cols + t) * bs
                    rows = pl.ds(i * bs, bs)
                    none = jnp.zeros_like(block)
                    mat_ref[rows, at : at + bs] = jnp.where(first, block, none)
                    mat_ref[rows, width + at : width + at + bs] = jnp.where(first, none, block)

    parts = factor_ref.shape[1]
    rows = factor_ref.shape[2] * factor_ref.shape[3]
    left = jnp.concatenate(
        [factor_ref[0, k].reshape(rows, factor_ref.shape[4]) for k in range(parts)], axis=1
    )
    total = jnp.dot(left, mat_ref[...], preferred_element_type=jnp.float32)
    out_ref[...] = jnp.zeros_like(out_ref)
    local_cols = out_ref.shape[0] // rows
    for n in range(2 * groups * cols):
        out_ref[pl.ds(info[head_count + n], rows, stride=local_cols), :] = total[
            :, n * bs : (n + 1) * bs
        ]


def local(basis_values, potential, basis_blocks, factor):
    row_count = lax.axis_size("row")
    col_count = lax.axis_size("col")
    group = lax.axis_index("groups")
    my_row = lax.axis_index("row")
    my_col = lax.axis_index("col")
    device_count = row_count * col_count
    phi = basis_values[0, 0]
    points, length = phi.shape
    block_list = basis_blocks[0, 0]
    list_length = block_list.shape[0]
    bs = factor.shape[2]
    total_blocks = NB // bs
    local_rows = total_blocks // row_count
    local_cols = total_blocks // col_count
    windows = total_blocks // WIN
    win_rows = WIN // row_count
    win_cols = WIN // col_count
    cols = win_cols // 2
    head_count = factor.shape[3] * col_count // bs
    params = functools.partial(pltpu.CompilerParams, vmem_limit_bytes=VMEM_LIMIT)

    half_rows = local_rows // 2
    my_half = lax.dynamic_slice_in_dim(factor[:, 0], group * half_rows, half_rows)
    factors = lax.all_gather(my_half, ("groups", "col"), axis=0)
    factors = factors.reshape(2, col_count, half_rows, bs, factor.shape[3])

    ahead = (block_list[None, :] - block_list[:, None]) % total_blocks
    is_first = jnp.all(ahead < WIN, axis=1)
    start = jnp.sum(jnp.where(is_first, block_list, 0))
    offset = start % WIN
    window = start // WIN

    position = (block_list - start) % total_blocks
    row_device = (offset + position) % row_count * col_count
    row_slot = position // row_count
    width = 2 * bs
    weight = potential[0, 0][:, None]
    received = []
    for t in range(cols):
        chosen = (group * cols + t) * col_count + jnp.arange(col_count)
        match = position[None, :] == chosen[:, None]
        list_index = jnp.sum(jnp.where(match, jnp.arange(list_length)[None, :], 0), axis=1)
        present = jnp.any(match, axis=1).astype(jnp.int32)
        col_device = (offset + chosen) % col_count
        info = jnp.concatenate(
            [list_index, present, col_device, row_device, row_slot, window[None]]
        ).astype(jnp.int32)
        extra = 16 if t == 0 else 0
        packed_shape = (device_count, win_rows * bs + extra, bs)
        packed = pl.pallas_call(
            functools.partial(pack_kernel, col_count, extra),
            out_shape=jax.ShapeDtypeStruct(packed_shape, jnp.bfloat16),
            grid_spec=pltpu.PrefetchScalarGridSpec(
                num_scalar_prefetch=1,
                grid=(length // width,),
                in_specs=[
                    pl.BlockSpec((points, width), lambda i, info: (0, i)),
                    pl.BlockSpec((points, 1), lambda i, info: (0, 0)),
                ]
                + [
                    pl.BlockSpec((points, bs), lambda i, info, j=j: (0, info[j]))
                    for j in range(col_count)
                ],
                out_specs=pl.BlockSpec(packed_shape, lambda i, info: (0, 0, 0)),
                scratch_shapes=[pltpu.VMEM((points, col_count * bs), jnp.bfloat16)],
            ),
            compiler_params=params(),
            cost_estimate=pl.CostEstimate(
                flops=2 * points * length * col_count * bs,
                bytes_accessed=4 * points * length,
                transcendentals=0,
            ),
        )(info, phi, weight, *([phi] * col_count))
        received.append(
            lax.all_to_all(
                packed,
                ("row", "col"),
                split_axis=0,
                concat_axis=0,
                tiled=True,
            )
        )

    rows_held = jnp.arange(local_rows) * row_count + my_row
    relative = (rows_held - offset) % total_blocks
    row_base = relative // WIN * win_rows + relative % WIN // row_count

    def held_cols(of_window, first, count):
        at = (first + jnp.arange(count)) * col_count + (my_col - offset) % col_count
        return (offset + WIN * of_window[:, None] + at[None, :]) % total_blocks // col_count

    row_window = relative // WIN
    head_rows = max(1, head_count // row_count)
    held = windows * win_rows
    window_of = received[0][:, win_rows * bs, 0].astype(jnp.int32)
    sum_info = jnp.concatenate([row_base[:head_rows], window_of])
    own_cols = [held_cols(row_window, group * cols + t, 1).reshape(-1) for t in range(cols)]
    other_cols = [
        held_cols(row_window, (1 - group) * cols + t, 1).reshape(-1) for t in range(cols)
    ]
    accs, heads, others, ahead_of_sum = [], [], [], []
    for t in range(cols):
        acc, narrow, head = pl.pallas_call(
            functools.partial(sum_kernel, head_rows, win_rows),
            out_shape=(
                jax.ShapeDtypeStruct((held, bs, bs), jnp.float32),
                jax.ShapeDtypeStruct((held, bs, bs), jnp.bfloat16),
                jax.ShapeDtypeStruct((head_rows, bs, bs), jnp.bfloat16),
            ),
            grid_spec=pltpu.PrefetchScalarGridSpec(
                num_scalar_prefetch=1,
                grid=(4,),
                in_specs=[
                    pl.BlockSpec(
                        (device_count // 4,) + received[t].shape[1:], lambda i, info: (i, 0, 0)
                    )
                ]
                + [pl.BlockSpec(memory_space=pl.ANY)] * len(ahead_of_sum),
                out_specs=(
                    pl.BlockSpec((held, bs, bs), lambda i, info: (0, 0, 0)),
                    pl.BlockSpec((held, bs, bs), lambda i, info: (0, 0, 0)),
                    pl.BlockSpec((head_rows, bs, bs), lambda i, info: (0, 0, 0)),
                ),
            ),
            compiler_params=params(),
            cost_estimate=pl.CostEstimate(
                flops=0, bytes_accessed=6 * 1024 * held * bs, transcendentals=0
            ),
        )(sum_info, received[t], *ahead_of_sum)
        gathered = lax.all_gather(head, ("groups", "row"), axis=0)
        heads.append(gathered.reshape(2, row_count, head_rows, bs, bs))
        accs.append(acc)
        others.append(lax.ppermute(narrow, "groups", [(0, 1), (1, 0)]))
        if t > 0:
            continue
        tile = pl.pallas_call(
            functools.partial(place_kernel, local_rows),
            out_shape=jax.ShapeDtypeStruct((local_rows, local_cols, bs, bs), jnp.float32),
            grid_spec=pltpu.PrefetchScalarGridSpec(
                num_scalar_prefetch=1,
                grid=(local_rows,),
                in_specs=[pl.BlockSpec((held, bs, bs), lambda i, info: (0, 0, 0))],
                out_specs=pl.BlockSpec((1, local_cols, bs, bs), lambda i, info: (i, 0, 0, 0)),
            ),
            compiler_params=params(),
            cost_estimate=pl.CostEstimate(
                flops=0, bytes_accessed=4 * local_rows * local_cols * bs * bs, transcendentals=0
            ),
        )(jnp.concatenate([row_base, own_cols[0]]), accs[0])
        ahead_of_sum = [tile, gathered, others[0]]

    fills = 2 * cols - 1
    tile = pl.pallas_call(
        functools.partial(fill_kernel, cols, cols - 1),
        out_shape=jax.ShapeDtypeStruct((local_rows, local_cols, bs, bs), jnp.float32),
        grid_spec=pltpu.PrefetchScalarGridSpec(
            num_scalar_prefetch=1,
            grid=(),
            in_specs=[pl.BlockSpec(memory_space=pltpu.VMEM)] * fills
            + [pl.BlockSpec(memory_space=pl.ANY)],
            out_specs=pl.BlockSpec(memory_space=pl.ANY),
            scratch_shapes=[
                pltpu.VMEM((cols, held, bs, bs), jnp.float32),
                pltpu.SemaphoreType.DMA((fills * local_rows,)),
            ],
        ),
        input_output_aliases={fills + 1: 0},
        compiler_params=params(),
    )(jnp.concatenate([row_base] + other_cols + own_cols[1:]), *others, *accs[1:], tile)

    head_window = (jnp.arange(head_count) - offset) % total_blocks // WIN
    in_first = (head_window == head_window[0]).astype(jnp.int32)
    pair = jnp.stack([head_window[0], (head_window[0] + 1) % windows])
    product_cols = held_cols(pair, 0, win_cols).reshape(-1)
    chunk = 2
    part_width = factor.shape[3]
    steps = half_rows // chunk
    product = pl.pallas_call(
        functools.partial(product_kernel, head_count, row_count, cols),
        out_shape=jax.ShapeDtypeStruct((local_rows * bs * local_cols, bs), jnp.float32),
        grid_spec=pltpu.PrefetchScalarGridSpec(
            num_scalar_prefetch=1,
            grid=(local_rows // chunk,),
            in_specs=[
                pl.BlockSpec(
                    (1, col_count, chunk, bs, part_width),
                    lambda i, info: (i // steps, 0, i % steps, 0, 0),
                ),
            ]
            + [pl.BlockSpec(heads[0].shape, lambda i, info: (0, 0, 0, 0, 0))] * cols,
            out_specs=pl.BlockSpec((chunk * bs * local_cols, bs), lambda i, info: (i, 0)),
            scratch_shapes=[pltpu.VMEM((head_count * bs, 2 * win_cols * bs), jnp.bfloat16)],
        ),
        compiler_params=params(),
    )(jnp.concatenate([in_first, product_cols]), factors, *heads)

    hamiltonian = tile.reshape(local_rows, 1, local_cols, 1, bs, bs)
    return hamiltonian, product.reshape(local_rows, 1, bs, local_cols, 1, bs)


def solution(mesh):
    return jax.shard_map(
        local,
        mesh=mesh,
        in_specs=(
            P("row", "col", None, None),
            P("row", "col", None),
            P("row", "col", None),
            P(None, "row", None, "col"),
        ),
        out_specs=(
            P("groups", "row", None, "col", None, None),
            P("groups", "row", None, None, "col", None),
        ),
        check_vma=False,
    )
```
